32 devices in a mesh: seq: 16 (over z, y, x), head: 2 (over core).
Axes of the slice: x: 2, y: 2, z: 4, core: 2. Of those that a mesh axis runs over, the one named last changes fastest.
Arguments:
- value_rows: bfloat16 [4096, 4096], P('seq', 'head'), may hold values from -6 to 6
- key_rows: bfloat16 [4096, 4096], P('seq', 'head'), may hold values from -6 to 6
- query_rows: bfloat16 [4096, 4096], P('seq', 'head'), may hold values from -6 to 6
- cotangent: bfloat16 [4096, 4096], P('seq', 'head'), may hold values from -6 to 6
- filter_taps: float32 [16, 2048], replicated, may hold values from -0.125 to 0.125
- doc_blocks: int32 [32], replicated, may hold values from 0 to 7, never falling along the last dimension, each value on 1 to 12 neighbouring positions
Outputs:
- output_rows: bfloat16 [4096, 4096], P('seq', 'head')
- grad_query: bfloat16 [4096, 4096], P('seq', 'head')
- grad_key: bfloat16 [4096, 4096], P('seq', 'head')
- grad_value: bfloat16 [4096, 4096], P('seq', 'head')
- grad_filter: float32 [16, 2048], replicated
The draws below stay inside these ranges and needn't reach their ends.
Inputs may be any that keep to these rules, and one draw needn't show every extreme that they name: doc_blocks gives each 128-token block its document number; numbers never fall, each document spans 1 to 12 blocks, and one spans exactly 12.
All inputs are finite; a program needn't handle non-finite values.
Results may differ from the reference program's by a relative error of at most 0.0058.
Values may be sent and summed in bfloat16 or wider, within the bound.
A program may use at most 384 MiB of HBM per device.

```python
import math
import jax
import jax.numpy as jnp
import numpy as np

H = 64
DH = 64
FILTERS = 16
K = 2048
BLK = 128
TOKENS = 4096
CH = 4096
NBLK = 32
DOCS = 8
MOST = 12


def levels(key, dims, shards, low, high):
    loudness, own = 1.0, jax.random.fold_in(key, 6)
    for axis_at, parts in shards:
        draws = jnp.exp(jax.random.uniform(jax.random.fold_in(own, axis_at), (parts,), jnp.float32, low / len(shards), high / len(shards)))
        loudness = loudness * jnp.repeat(draws, dims[axis_at] // parts).reshape([-1 if axis == axis_at else 1 for axis in range(len(dims))])
    return loudness


def split_up(amount, total, bound, skew):
    portions = [(1 << 20) // math.isqrt(rank ** skew) + 1 for rank in range(2, amount + 1)]
    rest, counts = total - bound - (amount - 1), [1] * (amount - 1)
    while rest > 0:
        free = [i for i in range(amount - 1) if counts[i] < bound]
        whole, remaining = sum([portions[i] for i in free]), rest
        for i in free:
            more = min(bound - counts[i], max(1, remaining * portions[i] // whole), rest)
            counts[i] = counts[i] + more
            rest = rest - more
    return np.array([bound] + counts)


def uneven_parts(key, number_of, total, bound, slope):
    if number_of == 2:
        one = jax.random.randint(key, (), max(1, total - bound), min(bound, total - 1) + 1)
        return jnp.stack([one, total - one])
    sizes = jnp.asarray(split_up(number_of, total, bound, slope), jnp.int32)
    couples = (number_of - 1) // 2
    donor, receiver = sizes[1:1 + 2 * couples:2], sizes[2:2 + 2 * couples:2]
    margin = jnp.minimum(donor - 1, bound - receiver)
    moved = jax.random.randint(jax.random.fold_in(key, 1), (couples,), 0, 1 << 20) % (margin + 1)
    sizes = sizes.at[1:1 + 2 * couples:2].set(donor - moved).at[2:2 + 2 * couples:2].set(receiver + moved)
    return sizes[jax.random.permutation(jax.random.fold_in(key, 2), number_of)]


def bell_draw(rng, dims, width, limit, split=(), held_as=jnp.bfloat16):
    values = jax.random.normal(rng, dims, jnp.float32) * width
    if len(split) > 0:
        values = levels(rng, dims, split, -0.22, 0.18) * values
    return jnp.clip(values, min=-limit, max=limit).astype(held_as)


def setup_inputs(seed: int = 0) -> dict:
    splits = jax.random.split(jax.random.key(seed), 7)
    value_rows = bell_draw(splits[0], (TOKENS, CH), 1.0, 6.0, ((0, 16), (1, 2)))
    key_rows = bell_draw(splits[1], (TOKENS, CH), 1.0, 6.0, ((0, 16), (1, 2)))
    query_rows = bell_draw(splits[2], (TOKENS, CH), 1.0, 6.0, ((0, 16), (1, 2)))
    cotangent = bell_draw(splits[3], (TOKENS, CH), 1.0, 6.0, ((0, 16), (1, 2)))
    filter_taps = bell_draw(splits[4], (FILTERS, K), K ** -0.5, 0.125, (), jnp.float32)
    doc_blocks = jnp.searchsorted(jnp.cumsum(uneven_parts(splits[5], DOCS, NBLK, MOST, 1)), jnp.arange(NBLK), side="right").astype(jnp.int32)
    return dict(value_rows=value_rows, key_rows=key_rows, query_rows=query_rows, cotangent=cotangent, filter_taps=filter_taps, doc_blocks=doc_blocks)


def toeplitz_blocks(filter_taps):
    lags_count = K // BLK + 1
    offsets = (jnp.arange(lags_count)[:, None, None] * BLK + jnp.arange(BLK)[None, :, None] - jnp.arange(BLK)[None, None, :]).astype(jnp.int32)
    inside = (offsets >= 0) & (offsets < K)
    safe_index = jnp.clip(offsets, 0, K - 1).astype(jnp.int32)
    rounded = filter_taps.astype(jnp.bfloat16)
    table = jnp.take(rounded, safe_index.reshape(-1), axis=1).reshape(FILTERS, lags_count, BLK, BLK)
    table = jnp.where(inside[None], table, jnp.zeros_like(table))
    return table, safe_index, inside


def reference(value_rows, key_rows, query_rows, cotangent, filter_taps, doc_blocks):
    blocks = TOKENS // BLK
    groups = H // FILTERS
    channels = H * DH
    lags_count = K // BLK + 1
    toeplitz, safe_index, inside = toeplitz_blocks(filter_taps)
    toeplitz_wide = toeplitz.astype(jnp.float32)
    product = (key_rows.astype(jnp.float32) * value_rows.astype(jnp.float32)).astype(jnp.bfloat16)
    scaled = (cotangent.astype(jnp.float32) * query_rows.astype(jnp.float32)).astype(jnp.bfloat16)
    shape5 = (blocks, BLK, groups, FILTERS, DH)
    past_blocks = product.astype(jnp.float32).reshape(shape5)
    fore_blocks = scaled.astype(jnp.float32).reshape(shape5)
    convolved = jnp.zeros(shape5, jnp.float32)
    adjoint = jnp.zeros(shape5, jnp.float32)
    grad_list = []
    for b in range(lags_count):
        filler = jnp.zeros((b, BLK, groups, FILTERS, DH), jnp.float32)
        source = jnp.concatenate([filler, past_blocks[:blocks - b]], 0)
        earlier = jnp.concatenate([jnp.full((b,), -1, jnp.int32), doc_blocks[:blocks - b]], 0)
        keep = (earlier == doc_blocks).astype(jnp.float32)
        source = source * keep[:, None, None, None, None]
        convolved = convolved + jnp.einsum('frs,nsgfd->nrgfd', toeplitz_wide[:, b], source)
        grad_list.append(jnp.einsum('nrgfd,nsgfd->frs', fore_blocks, source))
        later = jnp.concatenate([fore_blocks[b:], filler], 0)
        later_docs = jnp.concatenate([doc_blocks[b:], jnp.full((b,), -2, jnp.int32)], 0)
        keep_back = (later_docs == doc_blocks).astype(jnp.float32)
        later = later * keep_back[:, None, None, None, None]
        adjoint = adjoint + jnp.einsum('frs,nrgfd->nsgfd', toeplitz_wide[:, b], later)
    grad_blocks = jnp.stack(grad_list, 1)
    weighted = jnp.where(inside[None], grad_blocks, jnp.zeros_like(grad_blocks))
    grad_filter = jnp.zeros((FILTERS, K), jnp.float32).at[:, safe_index.reshape(-1)].add(weighted.reshape(FILTERS, -1))
    grad_filter = grad_filter / TOKENS
    convolved = convolved.reshape(TOKENS, channels)
    adjoint = adjoint.reshape(TOKENS, channels)
    output_rows = (query_rows.astype(jnp.float32) * convolved).astype(jnp.bfloat16)
    grad_query = (cotangent.astype(jnp.float32) * convolved).astype(jnp.bfloat16)
    grad_key = (adjoint * value_rows.astype(jnp.float32)).astype(jnp.bfloat16)
    grad_value = (adjoint * key_rows.astype(jnp.float32)).astype(jnp.bfloat16)
    return (output_rows, grad_query, grad_key, grad_value, grad_filter)
```

```python
import functools

import jax
import jax.numpy as jnp
from jax import lax
from jax.experimental import pallas as pl
from jax.experimental.pallas import tpu as pltpu
from jax.sharding import PartitionSpec as P

DH = 64
BLK = 128
MOST = 12
RANKS = 4
QUANTUM = 4
MESH = pl.DeviceIdType.MESH
ANY = pl.BlockSpec(memory_space=pl.ANY)


def wide(ref):
    return ref[...].astype(jnp.float32)


def prepare_kernel(groups, *refs):
    value, key = refs[:groups], refs[groups : 2 * groups]
    query, cot = refs[2 * groups : 3 * groups], refs[3 * groups : 4 * groups]
    product_ref, scaled_ref = refs[4 * groups :]
    for left, right, out in ((value, key, product_ref), (query, cot, scaled_ref)):
        parts = [wide(a) * wide(b) for a, b in zip(left, right)]
        for f in range(out.shape[0]):
            piece = jnp.concatenate([part[:, f * DH : (f + 1) * DH] for part in parts], 1)
            out[f] = piece.astype(jnp.bfloat16)


def prepare(value_rows, key_rows, query_rows, cotangent, filters):
    rows, channels = value_rows.shape
    groups = channels // (filters * DH)
    width = 4 * DH
    steps = filters // 4

    def spec(g):
        return pl.BlockSpec((rows, width), lambda p: (0, g * steps + p))

    specs = [spec(g) for g in range(groups)]
    args = []
    for array in (value_rows, key_rows, query_rows, cotangent):
        args += [array] * groups
    out = jax.ShapeDtypeStruct((filters, rows, groups * DH), jnp.bfloat16)
    out_spec = pl.BlockSpec((4, rows, groups * DH), lambda p: (p, 0, 0))
    return pl.pallas_call(
        functools.partial(prepare_kernel, groups),
        grid=(steps,),
        in_specs=specs * 4,
        out_specs=[out_spec, out_spec],
        out_shape=[out, out],
        compiler_params=pltpu.CompilerParams(vmem_limit_bytes=32 << 20),
    )(*args)


def finish_kernel(groups, conv, adj, value, key, query, cot, out, gq, gk, gv):
    for g in range(groups):

        @pl.when(pl.program_id(1) == g)
        def _():
            def joined(ref):
                parts = [
                    ref[f].astype(jnp.float32)[:, g * DH : (g + 1) * DH]
                    for f in range(ref.shape[0])
                ]
                return jnp.concatenate(parts, 1)

            convolved, adjoint = joined(conv), joined(adj)
            out[...] = (wide(query) * convolved).astype(jnp.bfloat16)
            gq[...] = (wide(cot) * convolved).astype(jnp.bfloat16)
            gk[...] = (wide(value) * adjoint).astype(jnp.bfloat16)
            gv[...] = (wide(key) * adjoint).astype(jnp.bfloat16)


def finish(conv, adj, value_rows, key_rows, query_rows, cotangent):
    filters, rows, cols = conv.shape
    groups = cols // DH
    steps = filters // 4
    spec = pl.BlockSpec((rows, 4 * DH), lambda p, g: (0, g * steps + p))
    back = pl.BlockSpec((4, rows, cols), lambda p, g: (p, 0, 0))
    shape = jax.ShapeDtypeStruct(value_rows.shape, jnp.bfloat16)
    return pl.pallas_call(
        functools.partial(finish_kernel, groups),
        grid=(steps, groups),
        in_specs=[back, back, spec, spec, spec, spec],
        out_specs=[spec] * 4,
        out_shape=[shape] * 4,
        compiler_params=pltpu.CompilerParams(vmem_limit_bytes=32 << 20),
    )(conv, adj, value_rows, key_rows, query_rows, cotangent)


def halo_parts(own, reach):
    parts, left, step = [], reach, 1
    while left > 0:
        parts.append((step, min(own, left)))
        left -= min(own, left)
        step += 1
    return parts


def spread_kernel(teams, reach, prod, scal, past, future, sends, recvs, far_sends, far_recvs, local_sems):
    per_rank, rows = prod.shape[1], prod.shape[2]
    own = RANKS * rows
    me = lax.axis_index("seq")
    rank, team = lax.rem(me, RANKS), lax.div(me, RANKS)
    halos = halo_parts(own, reach)
    barrier = pltpu.get_barrier_semaphore()
    peers = [team * RANKS + lax.rem(rank + k, RANKS) for k in range(1, RANKS)]
    for peer in peers:
        pl.semaphore_signal(barrier, inc=1, device_id={"seq": peer}, device_id_type=MESH)
    for k in range(1, teams):
        other = lax.rem(team + k, teams) * RANKS + rank
        pl.semaphore_signal(barrier, inc=1, device_id={"seq": other}, device_id_type=MESH)
    pl.semaphore_wait(barrier, RANKS + teams - 2)

    arrays = ((prod, past, reach), (scal, future, 0))
    at = pl.multiple_of(rank * rows, rows)

    def near(a, f, k):
        source, target, base = arrays[a]
        to = lax.rem(rank + k, RANKS)
        return pltpu.make_async_remote_copy(
            src_ref=source.at[to, f],
            dst_ref=target.at[f, pl.ds(base + at, rows)],
            send_sem=sends.at[a, f, k - 1],
            recv_sem=recvs.at[a, f, k - 1],
            device_id={"seq": team * RANKS + to},
            device_id_type=MESH,
        )

    def local(a, f):
        source, target, base = arrays[a]
        return pltpu.make_async_copy(
            source.at[rank, f], target.at[f, pl.ds(base + at, rows)], local_sems.at[a, f]
        )

    def far(a, f, h):
        step, size = halos[h]
        target = arrays[a][1]
        if a == 0:
            start = reach - (step - 1) * own - size
            src, dst, other = pl.ds(reach + own - size, size), pl.ds(start, size), me + step * RANKS
        else:
            src, dst, other = pl.ds(0, size), pl.ds(step * own, size), me - step * RANKS
        return pltpu.make_async_remote_copy(
            src_ref=target.at[f, src],
            dst_ref=target.at[f, dst],
            send_sem=far_sends.at[a, f, h],
            recv_sem=far_recvs.at[a, f, h],
            device_id={"seq": other},
            device_id_type=MESH,
        )

    def gives(a, h):
        step = halos[h][0]
        return team + step < teams if a == 0 else team - step >= 0

    def takes(a, h):
        step = halos[h][0]
        return team - step >= 0 if a == 0 else team + step < teams

    for f in range(per_rank):
        for a in range(2):
            local(a, f).start()
            for k in range(1, RANKS):
                near(a, f, k).start()
    for f in range(per_rank):
        for a in range(2):
            local(a, f).wait()
            for k in range(1, RANKS):
                near(a, f, k).wait_recv()
            for h in range(len(halos)):
                pl.when(gives(a, h))(lambda: far(a, f, h).start())
    for f in range(per_rank):
        for a in range(2):
            for k in range(1, RANKS):
                near(a, f, k).wait_send()
            for h in range(len(halos)):
                pl.when(gives(a, h))(lambda: far(a, f, h).wait_send())
                pl.when(takes(a, h))(lambda: far(a, f, h).wait_recv())


def spread(product, scaled, teams, reach):
    _, per_rank, rows, cols = product.shape
    out = jax.ShapeDtypeStruct((per_rank, RANKS * rows + reach, cols), jnp.bfloat16)
    halos = len(halo_parts(RANKS * rows, reach))
    return pl.pallas_call(
        functools.partial(spread_kernel, teams, reach),
        in_specs=[ANY, ANY],
        out_specs=[ANY, ANY],
        out_shape=[out, out],
        scratch_shapes=[
            pltpu.SemaphoreType.DMA((2, per_rank, RANKS - 1)),
            pltpu.SemaphoreType.DMA((2, per_rank, RANKS - 1)),
            pltpu.SemaphoreType.DMA((2, per_rank, halos)),
            pltpu.SemaphoreType.DMA((2, per_rank, halos)),
            pltpu.SemaphoreType.DMA((2, per_rank)),
        ],
        compiler_params=pltpu.CompilerParams(collective_id=0, has_side_effects=True),
    )(product, scaled)


def mix_kernel(back_len, fore_len, past_taps, fore_taps, past, future, conv, adj, grad, tp, tf, g_ref):
    cols = past.shape[2]
    own = conv.shape[1]
    reach = past.shape[1] - own
    span = tp.shape[1]
    lags = reach // BLK + 1
    for taps, strip in ((past_taps, tp), (fore_taps, tf)):
        rows = jnp.broadcast_to(taps[0], (BLK, span))
        strip[...] = pltpu.roll(rows, 0, 1, stride=1, stride_axis=0).astype(jnp.bfloat16)
    g_ref[...] = jnp.zeros_like(g_ref)
    i0 = lax.broadcasted_iota(jnp.int32, (BLK, BLK), 0)
    i1 = lax.broadcasted_iota(jnp.int32, (BLK, BLK), 1)
    mirror = (i0 + i1 == BLK - 1).astype(jnp.bfloat16)

    @pl.loop(0, own // BLK)
    def _(n):
        row = pl.multiple_of(n * BLK, BLK)
        lb, lf = back_len[n], fore_len[n]
        turned = jnp.dot(
            mirror, future[0, pl.ds(row, BLK)], preferred_element_type=jnp.float32
        ).astype(jnp.bfloat16)
        for size in range(QUANTUM, lags + 1, QUANTUM):
            wide_by = size * BLK
            at = lax.broadcasted_iota(jnp.int32, (wide_by, cols), 0)

            @pl.when((lb <= size) & (lb > size - QUANTUM))
            def _():
                first = pl.multiple_of(row + reach + BLK - wide_by, BLK)
                x = past[0, pl.ds(first, wide_by)]
                x = jnp.where(at >= (size - lb) * BLK, x, jnp.zeros_like(x))
                low = (lags - size) * BLK
                sums = jnp.dot(
                    tp[:, low : lags * BLK], x, preferred_element_type=jnp.float32
                )
                conv[0, pl.ds(row, BLK)] = sums.astype(jnp.bfloat16)
                g_ref[:, low : lags * BLK] += lax.dot_general(
                    turned, x, (((1,), (1,)), ((), ())), preferred_element_type=jnp.float32
                )

            @pl.when((lf <= size) & (lf > size - QUANTUM))
            def _():
                x = future[0, pl.ds(row, wide_by)]
                x = jnp.where(at < lf * BLK, x, jnp.zeros_like(x))
                sums = jnp.dot(tf[:, :wide_by], x, preferred_element_type=jnp.float32)
                adj[0, pl.ds(row, BLK)] = sums.astype(jnp.bfloat16)

    aligned = pltpu.roll(g_ref[...], 0, 1, stride=1, stride_axis=0)
    grad[0] = jnp.sum(aligned, 0, keepdims=True)


def mix(back_len, fore_len, past_taps, fore_taps, past, future, own):
    per_rank, rows, cols = past.shape
    span = past_taps.shape[2]

    def spec(*dims):
        return pl.BlockSpec((1,) + dims, lambda f, *_: (f, 0, 0))

    out = jax.ShapeDtypeStruct((per_rank, own, cols), jnp.bfloat16)
    return pl.pallas_call(
        mix_kernel,
        grid_spec=pltpu.PrefetchScalarGridSpec(
            num_scalar_prefetch=2,
            grid=(per_rank,),
            in_specs=[spec(1, span), spec(1, span), spec(rows, cols), spec(rows, cols)],
            out_specs=[spec(own, cols), spec(own, cols), spec(1, span)],
            scratch_shapes=[
                pltpu.VMEM((BLK, span), jnp.bfloat16),
                pltpu.VMEM((BLK, span), jnp.bfloat16),
                pltpu.VMEM((BLK, span), jnp.float32),
            ],
        ),
        out_shape=[out, out, jax.ShapeDtypeStruct((per_rank, 1, span), jnp.float32)],
        compiler_params=pltpu.CompilerParams(vmem_limit_bytes=48 << 20),
    )(back_len, fore_len, past_taps, fore_taps, past, future)


def gather_kernel(teams, heads, conv, adj, grad, conv_all, adj_all, grad_all, slots, sends, recvs, g_sends, g_recvs, s_sends, s_recvs, local_sems):
    rows = conv_all.shape[2]
    me, head = lax.axis_index("seq"), lax.axis_index("head")
    rank, team = lax.rem(me, RANKS), lax.div(me, RANKS)
    barrier = pltpu.get_barrier_semaphore()
    ring = [(t, h) for t in range(teams) for h in range(heads)][1:]

    def mate(t, h):
        return {
            "seq": lax.rem(team + t, teams) * RANKS + rank,
            "head": lax.rem(head + h, heads),
        }

    def near_id(k):
        return {"seq": team * RANKS + lax.rem(rank + k, RANKS), "head": head}

    for k in range(1, RANKS):
        pl.semaphore_signal(barrier, inc=1, device_id=near_id(k), device_id_type=MESH)
    for t, h in ring:
        pl.semaphore_signal(barrier, inc=1, device_id=mate(t, h), device_id_type=MESH)
    pl.semaphore_wait(barrier, RANKS - 1 + len(ring))

    def sum_copy(i):
        return pltpu.make_async_remote_copy(
            src_ref=grad,
            dst_ref=slots.at[i],
            send_sem=g_sends.at[i],
            recv_sem=g_recvs.at[i],
            device_id=mate(*ring[i]),
            device_id_type=MESH,
        )

    def near(a, k):
        source, target = ((conv, conv_all), (adj, adj_all))[a]
        to = lax.rem(rank + k, RANKS)
        return pltpu.make_async_remote_copy(
            src_ref=source.at[:, pl.ds(pl.multiple_of(to * rows, rows), rows)],
            dst_ref=target.at[rank],
            send_sem=sends.at[a, k - 1],
            recv_sem=recvs.at[a, k - 1],
            device_id=near_id(k),
            device_id_type=MESH,
        )

    def local(a):
        source, target = ((conv, conv_all), (adj, adj_all))[a]
        return pltpu.make_async_copy(
            source.at[:, pl.ds(pl.multiple_of(rank * rows, rows), rows)],
            target.at[rank],
            local_sems.at[a],
        )

    def share(k):
        return pltpu.make_async_remote_copy(
            src_ref=grad_all.at[rank],
            dst_ref=grad_all.at[rank],
            send_sem=s_sends.at[k - 1],
            recv_sem=s_recvs.at[k - 1],
            device_id=near_id(k),
            device_id_type=MESH,
        )

    for i in range(len(ring)):
        sum_copy(i).start()
    for a in range(2):
        local(a).start()
        for k in range(1, RANKS):
            near(a, k).start()
    total = grad[...]
    for i in range(len(ring)):
        sum_copy(i).wait_recv()
    for i in range(len(ring)):
        total = total + slots[i]
    grad_all[rank] = total
    for k in range(1, RANKS):
        share(k).start()
    for i in range(len(ring)):
        sum_copy(i).wait_send()
    for a in range(2):
        local(a).wait()
        for k in range(1, RANKS):
            near(a, k).wait()
    for k in range(1, RANKS):
        share(k).wait()


def gather(conv, adj, grad, teams, heads):
    per_rank, own, cols = conv.shape
    out = jax.ShapeDtypeStruct((RANKS, per_rank, own // RANKS, cols), jnp.bfloat16)
    others = teams * heads - 1
    vmem = pl.BlockSpec(memory_space=pltpu.VMEM)
    dma = pltpu.SemaphoreType.DMA
    return pl.pallas_call(
        functools.partial(gather_kernel, teams, heads),
        in_specs=[ANY, ANY, vmem],
        out_specs=[ANY, ANY, vmem],
        out_shape=[out, out, jax.ShapeDtypeStruct((RANKS,) + grad.shape, jnp.float32)],
        scratch_shapes=[
            pltpu.VMEM((others,) + grad.shape, jnp.float32),
            dma((2, RANKS - 1)),
            dma((2, RANKS - 1)),
            dma((others,)),
            dma((others,)),
            dma((RANKS - 1,)),
            dma((RANKS - 1,)),
            dma((2,)),
        ],
        compiler_params=pltpu.CompilerParams(
            collective_id=1, has_side_effects=True, vmem_limit_bytes=32 << 20
        ),
    )(conv, adj, grad)


def per_device(value_rows, key_rows, query_rows, cotangent, filter_taps, doc_blocks):
    rows, channels = value_rows.shape
    filters, taps_total = filter_taps.shape
    cols = channels // filters
    per_rank = filters // RANKS
    seq, heads = lax.axis_size("seq"), lax.axis_size("head")
    teams = seq // RANKS
    own = RANKS * rows
    own_blocks = own // BLK
    lags = min(MOST, taps_total // BLK)
    reach = (lags - 1) * BLK
    used = lags * BLK
    me = lax.axis_index("seq")
    rank, team = lax.rem(me, RANKS), lax.div(me, RANKS)

    product, scaled = prepare(value_rows, key_rows, query_rows, cotangent, filters)
    shape = (RANKS, per_rank, rows, cols)
    past, future = spread(product.reshape(shape), scaled.reshape(shape), teams, reach)

    mine = lax.dynamic_slice_in_dim(filter_taps, rank * per_rank, per_rank, 0)[:, :used]
    mine = mine.astype(jnp.bfloat16).astype(jnp.float32)
    turned = mine[:, ::-1]
    gap = jnp.zeros((per_rank, BLK), jnp.float32)
    past_taps = jnp.concatenate([turned[:, BLK - 1 :], gap, turned[:, : BLK - 1]], 1)
    fore_taps = jnp.concatenate([mine, gap], 1)

    fill = jnp.full((lags - 1,), -1, jnp.int32)
    docs = jnp.concatenate([fill, doc_blocks, fill - 1], 0)
    window = lax.dynamic_slice_in_dim(docs, team * own_blocks, own_blocks + 2 * (lags - 1))
    here = window[lags - 1 : lags - 1 + own_blocks]
    back_len = sum(
        (window[lags - 1 - b : lags - 1 - b + own_blocks] == here).astype(jnp.int32)
        for b in range(lags)
    )
    fore_len = sum(
        (window[lags - 1 + b : lags - 1 + b + own_blocks] == here).astype(jnp.int32)
        for b in range(lags)
    )
    conv, adj, grad = mix(
        back_len, fore_len, past_taps[:, None], fore_taps[:, None], past, future, own
    )
    conv_all, adj_all, grad_all = gather(
        conv, adj, jnp.pad(grad[:, 0, :used], ((0, 0), (0, taps_total - used))).reshape(-1, BLK),
        teams, heads,
    )
    whole = (filters, rows, cols)
    outs = finish(
        conv_all.reshape(whole), adj_all.reshape(whole), value_rows, key_rows, query_rows, cotangent
    )
    taps_grad = grad_all.reshape(filters, taps_total)[:, :used][:, ::-1]
    taps_grad = jnp.pad(taps_grad, ((0, 0), (0, taps_total - used)))
    return (*outs, taps_grad * (1.0 / (rows * seq)))


def solution(mesh):
    rows = P("seq", "head")
    return jax.shard_map(
        per_device,
        mesh=mesh,
        in_specs=(rows, rows, rows, rows, P(), P()),
        out_specs=(rows, rows, rows, rows, P()),
        check_vma=False,
    )
```

```python
import functools

import jax
import jax.numpy as jnp
from jax import lax
from jax.experimental import pallas as pl
from jax.experimental.pallas import tpu as pltpu
from jax.sharding import PartitionSpec as P

DH = 64
BLK = 128
MOST = 12
RANKS = 4
MESH = pl.DeviceIdType.MESH
ANY = pl.BlockSpec(memory_space=pl.ANY)


def wide(ref):
    return ref[...].astype(jnp.float32)


def prepare_kernel(groups, *refs):
    value, key = refs[:groups], refs[groups : 2 * groups]
    query, cot = refs[2 * groups : 3 * groups], refs[3 * groups : 4 * groups]
    product_ref, scaled_ref = refs[4 * groups :]
    for left, right, out in ((value, key, product_ref), (query, cot, scaled_ref)):
        parts = [wide(a) * wide(b) for a, b in zip(left, right)]
        for f in range(out.shape[0]):
            piece = jnp.concatenate([part[:, f * DH : (f + 1) * DH] for part in parts], 1)
            out[f] = piece.astype(jnp.bfloat16)


def prepare(value_rows, key_rows, query_rows, cotangent, filters):
    rows, channels = value_rows.shape
    groups = channels // (filters * DH)
    width = 4 * DH
    steps = filters // 4

    def spec(g):
        return pl.BlockSpec((rows, width), lambda p: (0, g * steps + p))

    specs = [spec(g) for g in range(groups)]
    args = []
    for array in (value_rows, key_rows, query_rows, cotangent):
        args += [array] * groups
    out = jax.ShapeDtypeStruct((filters, rows, groups * DH), jnp.bfloat16)
    out_spec = pl.BlockSpec((4, rows, groups * DH), lambda p: (p, 0, 0))
    return pl.pallas_call(
        functools.partial(prepare_kernel, groups),
        grid=(steps,),
        in_specs=specs * 4,
        out_specs=[out_spec, out_spec],
        out_shape=[out, out],
        compiler_params=pltpu.CompilerParams(vmem_limit_bytes=56 << 20),
    )(*args)


def finish_kernel(groups, conv, adj, value, key, query, cot, out, gq, gk, gv):
    for g in range(groups):

        @pl.when(pl.program_id(1) == g)
        def _():
            def joined(ref):
                parts = [
                    ref[f].astype(jnp.float32)[:, g * DH : (g + 1) * DH]
                    for f in range(ref.shape[0])
                ]
                return jnp.concatenate(parts, 1)

            convolved, adjoint = joined(conv), joined(adj)
            out[...] = (wide(query) * convolved).astype(jnp.bfloat16)
            gq[...] = (wide(cot) * convolved).astype(jnp.bfloat16)
            gk[...] = (wide(value) * adjoint).astype(jnp.bfloat16)
            gv[...] = (wide(key) * adjoint).astype(jnp.bfloat16)


def finish(conv, adj, value_rows, key_rows, query_rows, cotangent):
    filters, rows, cols = conv.shape
    groups = cols // DH
    steps = filters // 4
    spec = pl.BlockSpec((rows, 4 * DH), lambda p, g: (0, g * steps + p))
    back = pl.BlockSpec((4, rows, cols), lambda p, g: (p, 0, 0))
    shape = jax.ShapeDtypeStruct(value_rows.shape, jnp.bfloat16)
    return pl.pallas_call(
        functools.partial(finish_kernel, groups),
        grid=(steps, groups),
        in_specs=[back, back, spec, spec, spec, spec],
        out_specs=[spec] * 4,
        out_shape=[shape] * 4,
        compiler_params=pltpu.CompilerParams(vmem_limit_bytes=56 << 20),
    )(conv, adj, value_rows, key_rows, query_rows, cotangent)


def halo_parts(own, reach):
    parts, left, step = [], reach, 1
    while left > 0:
        parts.append((step, min(own, left)))
        left -= min(own, left)
        step += 1
    return parts


def mix_kernel(
    teams, heads, reach, back_len, fore_len, past_taps, fore_taps, prod, scal,
    conv_all, adj_all, grad_all,
    past, future, tp, tf, g_ref, conv, adj, grad, slots,
    sends, recvs, far_sends, far_recvs, out_sends, out_recvs, g_sends, g_recvs, s_sends, s_recvs,
    local_sems, out_local,
):
    _, per_rank, rows, cols = prod.shape
    own = RANKS * rows
    span = tp.shape[2]
    used = span - BLK
    lines = grad.shape[1]
    me, head = lax.axis_index("seq"), lax.axis_index("head")
    rank, team = lax.rem(me, RANKS), lax.div(me, RANKS)
    halos = halo_parts(own, reach)
    ring = [(t, h) for t in range(teams) for h in range(heads)][1:]
    arrays = ((prod, past, reach), (scal, future, 0))
    returns = ((conv, conv_all), (adj, adj_all))
    at = pl.multiple_of(rank * rows, rows)

    def mate(t, h):
        return {
            "seq": lax.rem(team + t, teams) * RANKS + rank,
            "head": lax.rem(head + h, heads),
        }

    def near_id(k):
        return {"seq": team * RANKS + lax.rem(rank + k, RANKS), "head": head}

    barrier = pltpu.get_barrier_semaphore()
    for k in range(1, RANKS):
        pl.semaphore_signal(barrier, inc=1, device_id=near_id(k), device_id_type=MESH)
    for t, h in ring:
        pl.semaphore_signal(barrier, inc=1, device_id=mate(t, h), device_id_type=MESH)
    pl.semaphore_wait(barrier, RANKS - 1 + len(ring))

    def near(a, f, k):
        source, target, base = arrays[a]
        return pltpu.make_async_remote_copy(
            src_ref=source.at[lax.rem(rank + k, RANKS), f],
            dst_ref=target.at[f, pl.ds(base + at, rows)],
            send_sem=sends.at[a, f, k - 1],
            recv_sem=recvs.at[a, f, k - 1],
            device_id=near_id(k),
            device_id_type=MESH,
        )

    def local(a, f):
        source, target, base = arrays[a]
        return pltpu.make_async_copy(
            source.at[rank, f], target.at[f, pl.ds(base + at, rows)], local_sems.at[a, f]
        )

    def far(a, f, h):
        step, size = halos[h]
        target = arrays[a][1]
        if a == 0:
            start = reach - (step - 1) * own - size
            src, dst, other = pl.ds(reach + own - size, size), pl.ds(start, size), me + step * RANKS
        else:
            src, dst, other = pl.ds(0, size), pl.ds(step * own, size), me - step * RANKS
        return pltpu.make_async_remote_copy(
            src_ref=target.at[f, src],
            dst_ref=target.at[f, dst],
            send_sem=far_sends.at[a, f, h],
            recv_sem=far_recvs.at[a, f, h],
            device_id={"seq": other, "head": head},
            device_id_type=MESH,
        )

    def gives(a, h):
        step = halos[h][0]
        return team + step < teams if a == 0 else team - step >= 0

    def takes(a, h):
        step = halos[h][0]
        return team - step >= 0 if a == 0 else team + step < teams

    def back(a, f, k):
        source, target = returns[a]
        to = lax.rem(rank + k, RANKS)
        return pltpu.make_async_remote_copy(
            src_ref=source.at[f, pl.ds(pl.multiple_of(to * rows, rows), rows)],
            dst_ref=target.at[rank, f],
            send_sem=out_sends.at[a, f, k - 1],
            recv_sem=out_recvs.at[a, f, k - 1],
            device_id=near_id(k),
            device_id_type=MESH,
        )

    def back_local(a, f):
        source, target = returns[a]
        return pltpu.make_async_copy(
            source.at[f, pl.ds(at, rows)], target.at[rank, f], out_local.at[a, f]
        )

    def sum_copy(i, f):
        return pltpu.make_async_remote_copy(
            src_ref=grad.at[f],
            dst_ref=slots.at[i, f],
            send_sem=g_sends.at[i, f],
            recv_sem=g_recvs.at[i, f],
            device_id=mate(*ring[i]),
            device_id_type=MESH,
        )

    def share(k):
        return pltpu.make_async_remote_copy(
            src_ref=grad_all.at[rank],
            dst_ref=grad_all.at[rank],
            send_sem=s_sends.at[k - 1],
            recv_sem=s_recvs.at[k - 1],
            device_id=near_id(k),
            device_id_type=MESH,
        )

    for f in range(per_rank):
        for a in range(2):
            for k in range(1, RANKS):
                near(a, f, k).start()
            local(a, f).start()

    @pl.loop(0, per_rank)
    def _(f):
        for taps, strip in ((past_taps, tp), (fore_taps, tf)):
            lines_all = jnp.broadcast_to(taps[f], (BLK, span))
            turned = pltpu.roll(lines_all, 0, 1, stride=1, stride_axis=0)
            strip[f] = turned.astype(jnp.bfloat16)

    grad[...] = jnp.zeros_like(grad)

    for f in range(per_rank):
        for a in range(2):
            local(a, f).wait()
            for k in range(1, RANKS):
                near(a, f, k).wait_recv()
            for h in range(len(halos)):
                pl.when(gives(a, h))(lambda: far(a, f, h).start())

    i0 = lax.broadcasted_iota(jnp.int32, (BLK, BLK), 0)
    i1 = lax.broadcasted_iota(jnp.int32, (BLK, BLK), 1)
    mirror = (i0 + i1 == BLK - 1).astype(jnp.bfloat16)

    @pl.loop(0, per_rank)
    def _(f):
        for a in range(2):
            for h in range(len(halos)):
                pl.when(takes(a, h))(lambda: far(a, f, h).wait_recv())
        g_ref[...] = jnp.zeros_like(g_ref)

        @pl.loop(0, own // (2 * BLK))
        def _(pair):
            starts = [pl.multiple_of(pair * 2 * BLK + i * BLK, BLK) for i in range(2)]
            place = lax.broadcasted_iota(jnp.int32, (used, cols), 0)
            xs, ys, ss = [], [], []
            for i in range(2):
                low = used - back_len[pair * 2 + i] * BLK
                high = fore_len[pair * 2 + i] * BLK
                x = past[f, pl.ds(starts[i], used)]
                xs.append(jnp.where(place >= low, x, jnp.zeros_like(x)))
                y = future[f, pl.ds(starts[i], used)]
                ys.append(jnp.where(place < high, y, jnp.zeros_like(y)))
                ss.append(y[:BLK])
            x2, y2, s2 = [jnp.concatenate(parts, 1) for parts in (xs, ys, ss)]
            ahead = jnp.dot(tp[f, :, :used], x2, preferred_element_type=jnp.float32)
            after = jnp.dot(tf[f, :, :used], y2, preferred_element_type=jnp.float32)
            flipped = jnp.dot(mirror, s2, preferred_element_type=jnp.float32)
            g_ref[:, :used] += lax.dot_general(
                flipped.astype(jnp.bfloat16),
                x2,
                (((1,), (1,)), ((), ())),
                preferred_element_type=jnp.float32,
            )
            for i in range(2):
                part = slice(i * cols, (i + 1) * cols)
                conv[f, pl.ds(starts[i], BLK)] = ahead[:, part].astype(jnp.bfloat16)
                adj[f, pl.ds(starts[i], BLK)] = after[:, part].astype(jnp.bfloat16)

        for a in range(2):
            for k in range(1, RANKS):
                back(a, f, k).start()
            back_local(a, f).start()
        aligned = pltpu.roll(g_ref[...], 0, 1, stride=1, stride_axis=0)
        sums = jnp.sum(aligned, 0, keepdims=True)
        for c in range(used // BLK):
            grad[f, c : c + 1] = sums[:, c * BLK : (c + 1) * BLK]
        for i in range(len(ring)):
            sum_copy(i, f).start()

    for i in range(len(ring)):
        for f in range(per_rank):
            sum_copy(i, f).wait_recv()
    total = grad[...]
    for i in range(len(ring)):
        total = total + slots[i]
    grad_all[rank] = total
    for k in range(1, RANKS):
        share(k).start()
    for f in range(per_rank):
        for a in range(2):
            for k in range(1, RANKS):
                near(a, f, k).wait_send()
            for h in range(len(halos)):
                pl.when(gives(a, h))(lambda: far(a, f, h).wait_send())
        for i in range(len(ring)):
            sum_copy(i, f).wait_send()
        for a in range(2):
            back_local(a, f).wait()
            for k in range(1, RANKS):
                back(a, f, k).wait()
    for k in range(1, RANKS):
        share(k).wait()


def mix(back_len, fore_len, past_taps, fore_taps, product, scaled, teams, heads, lines):
    _, per_rank, rows, cols = product.shape
    own = RANKS * rows
    span = past_taps.shape[2]
    reach = span - 2 * BLK
    others = teams * heads - 1
    halos = len(halo_parts(own, reach))
    vmem = pl.BlockSpec(memory_space=pltpu.VMEM)
    smem = pl.BlockSpec(memory_space=pltpu.SMEM)
    dma = pltpu.SemaphoreType.DMA
    out = jax.ShapeDtypeStruct((RANKS, per_rank, rows, cols), jnp.bfloat16)
    held = pltpu.VMEM((per_rank, own + reach, cols), jnp.bfloat16)
    strip = pltpu.VMEM((per_rank, BLK, span), jnp.bfloat16)
    result = pltpu.VMEM((per_rank, own, cols), jnp.bfloat16)
    grads = (per_rank, lines, BLK)
    return pl.pallas_call(
        functools.partial(mix_kernel, teams, heads, reach),
        in_specs=[smem, smem, vmem, vmem, ANY, ANY],
        out_specs=[ANY, ANY, vmem],
        out_shape=[out, out, jax.ShapeDtypeStruct((RANKS,) + grads, jnp.float32)],
        scratch_shapes=[
            held,
            held,
            strip,
            strip,
            pltpu.VMEM((BLK, span), jnp.float32),
            result,
            result,
            pltpu.VMEM(grads, jnp.float32),
            pltpu.VMEM((others,) + grads, jnp.float32),
            dma((2, per_rank, RANKS - 1)),
            dma((2, per_rank, RANKS - 1)),
            dma((2, per_rank, halos)),
            dma((2, per_rank, halos)),
            dma((2, per_rank, RANKS - 1)),
            dma((2, per_rank, RANKS - 1)),
            dma((others, per_rank)),
            dma((others, per_rank)),
            dma((RANKS - 1,)),
            dma((RANKS - 1,)),
            dma((2, per_rank)),
            dma((2, per_rank)),
        ],
        compiler_params=pltpu.CompilerParams(
            collective_id=0, has_side_effects=True, vmem_limit_bytes=56 << 20
        ),
    )(back_len, fore_len, past_taps, fore_taps, product, scaled)


def per_device(value_rows, key_rows, query_rows, cotangent, filter_taps, doc_blocks):
    rows, channels = value_rows.shape
    filters, taps_total = filter_taps.shape
    cols = channels // filters
    per_rank = filters // RANKS
    seq, heads = lax.axis_size("seq"), lax.axis_size("head")
    teams = seq // RANKS
    own = RANKS * rows
    own_blocks = own // BLK
    lags = min(MOST, taps_total // BLK)
    used = lags * BLK
    me = lax.axis_index("seq")
    rank, team = lax.rem(me, RANKS), lax.div(me, RANKS)

    product, scaled = prepare(value_rows, key_rows, query_rows, cotangent, filters)
    shape = (RANKS, per_rank, rows, cols)
    mine = lax.dynamic_slice_in_dim(filter_taps, rank * per_rank, per_rank, 0)[:, :used]
    mine = mine.astype(jnp.bfloat16).astype(jnp.float32)
    turned = mine[:, ::-1]
    gap = jnp.zeros((per_rank, BLK), jnp.float32)
    past_taps = jnp.concatenate([turned[:, BLK - 1 :], gap, turned[:, : BLK - 1]], 1)
    fore_taps = jnp.concatenate([mine, gap], 1)

    fill = jnp.full((lags - 1,), -1, jnp.int32)
    docs = jnp.concatenate([fill, doc_blocks, fill - 1], 0)
    window = lax.dynamic_slice_in_dim(docs, team * own_blocks, own_blocks + 2 * (lags - 1))
    here = window[lags - 1 : lags - 1 + own_blocks]
    back_len = sum(
        (window[lags - 1 - b : lags - 1 - b + own_blocks] == here).astype(jnp.int32)
        for b in range(lags)
    )
    fore_len = sum(
        (window[lags - 1 + b : lags - 1 + b + own_blocks] == here).astype(jnp.int32)
        for b in range(lags)
    )
    conv_all, adj_all, grad_all = mix(
        back_len, fore_len, past_taps[:, None], fore_taps[:, None],
        product.reshape(shape), scaled.reshape(shape), teams, heads, taps_total // BLK,
    )
    whole = (filters, rows, cols)
    outs = finish(
        conv_all.reshape(whole), adj_all.reshape(whole), value_rows, key_rows, query_rows, cotangent
    )
    taps_grad = grad_all.reshape(filters, taps_total)[:, :used][:, ::-1]
    taps_grad = jnp.pad(taps_grad, ((0, 0), (0, taps_total - used)))
    return (*outs, taps_grad * (1.0 / (rows * seq)))


def solution(mesh):
    rows = P("seq", "head")
    return jax.shard_map(
        per_device,
        mesh=mesh,
        in_specs=(rows, rows, rows, rows, P(), P()),
        out_specs=(rows, rows, rows, rows, P()),
        check_vma=False,
    )
```

```python
import functools

import jax
import jax.numpy as jnp
from jax import lax
from jax.experimental import pallas as pl
from jax.experimental.pallas import tpu as pltpu
from jax.sharding import PartitionSpec as P

DH = 64
BLK = 128
MOST = 12
RANKS = 4
MESH = pl.DeviceIdType.MESH
ANY = pl.BlockSpec(memory_space=pl.ANY)


def wide(ref):
    return ref[...].astype(jnp.float32)


def prepare_kernel(groups, *refs):
    value, key = refs[:groups], refs[groups : 2 * groups]
    query, cot = refs[2 * groups : 3 * groups], refs[3 * groups : 4 * groups]
    product_ref, scaled_ref = refs[4 * groups :]
    for left, right, out in ((value, key, product_ref), (query, cot, scaled_ref)):
        parts = [wide(a) * wide(b) for a, b in zip(left, right)]
        for f in range(out.shape[0]):
            piece = jnp.concatenate([part[:, f * DH : (f + 1) * DH] for part in parts], 1)
            out[f] = piece.astype(jnp.bfloat16)


def prepare(value_rows, key_rows, query_rows, cotangent, filters):
    rows, channels = value_rows.shape
    groups = channels // (filters * DH)
    width = 4 * DH
    steps = filters // 4

    def spec(g):
        return pl.BlockSpec((rows, width), lambda p: (0, g * steps + p))

    specs = [spec(g) for g in range(groups)]
    args = []
    for array in (value_rows, key_rows, query_rows, cotangent):
        args += [array] * groups
    out = jax.ShapeDtypeStruct((filters, rows, groups * DH), jnp.bfloat16)
    out_spec = pl.BlockSpec((4, rows, groups * DH), lambda p: (p, 0, 0))
    return pl.pallas_call(
        functools.partial(prepare_kernel, groups),
        grid=(steps,),
        in_specs=specs * 4,
        out_specs=[out_spec, out_spec],
        out_shape=[out, out],
        compiler_params=pltpu.CompilerParams(vmem_limit_bytes=56 << 20),
    )(*args)


def finish_kernel(groups, conv, adj, value, key, query, cot, out, gq, gk, gv):
    for g in range(groups):

        @pl.when(pl.program_id(1) == g)
        def _():
            def joined(ref):
                parts = [
                    ref[f].astype(jnp.float32)[:, g * DH : (g + 1) * DH]
                    for f in range(ref.shape[0])
                ]
                return jnp.concatenate(parts, 1)

            convolved, adjoint = joined(conv), joined(adj)
            out[...] = (wide(query) * convolved).astype(jnp.bfloat16)
            gq[...] = (wide(cot) * convolved).astype(jnp.bfloat16)
            gk[...] = (wide(value) * adjoint).astype(jnp.bfloat16)
            gv[...] = (wide(key) * adjoint).astype(jnp.bfloat16)


def finish(conv, adj, value_rows, key_rows, query_rows, cotangent):
    filters, rows, cols = conv.shape
    groups = cols // DH
    steps = filters // 4
    spec = pl.BlockSpec((rows, 4 * DH), lambda p, g: (0, g * steps + p))
    back = pl.BlockSpec((4, rows, cols), lambda p, g: (p, 0, 0))
    shape = jax.ShapeDtypeStruct(value_rows.shape, jnp.bfloat16)
    return pl.pallas_call(
        functools.partial(finish_kernel, groups),
        grid=(steps, groups),
        in_specs=[back, back, spec, spec, spec, spec],
        out_specs=[spec] * 4,
        out_shape=[shape] * 4,
        compiler_params=pltpu.CompilerParams(vmem_limit_bytes=56 << 20),
    )(conv, adj, value_rows, key_rows, query_rows, cotangent)


def halo_parts(own, reach):
    parts, left, step = [], reach, 1
    while left > 0:
        parts.append((step, min(own, left)))
        left -= min(own, left)
        step += 1
    return parts


def mix_kernel(
    teams, heads, reach, back_len, fore_len, past_taps, fore_taps, prod, scal,
    conv_all, adj_all, grad_all,
    past, future, tp, tf, g_ref, conv, adj, grad, slots,
    sends, recvs, far_sends, far_recvs, out_sends, out_recvs, g_sends, g_recvs, s_sends, s_recvs,
    local_sems, out_local,
):
    _, per_rank, rows, cols = prod.shape
    own = RANKS * rows
    span = tp.shape[2]
    used = span - BLK
    lines = grad.shape[1]
    me, head = lax.axis_index("seq"), lax.axis_index("head")
    rank, team = lax.rem(me, RANKS), lax.div(me, RANKS)
    halos = halo_parts(own, reach)
    ring = [(t, h) for t in range(teams) for h in range(heads)][1:]
    arrays = ((prod, past, reach), (scal, future, 0))
    returns = ((conv, conv_all), (adj, adj_all))
    at = pl.multiple_of(rank * rows, rows)

    def mate(t, h):
        return {
            "seq": lax.rem(team + t, teams) * RANKS + rank,
            "head": lax.rem(head + h, heads),
        }

    def near_id(k):
        return {"seq": team * RANKS + lax.rem(rank + k, RANKS), "head": head}

    barrier = pltpu.get_barrier_semaphore()
    for k in range(1, RANKS):
        pl.semaphore_signal(barrier, inc=1, device_id=near_id(k), device_id_type=MESH)
    for t, h in ring:
        pl.semaphore_signal(barrier, inc=1, device_id=mate(t, h), device_id_type=MESH)
    pl.semaphore_wait(barrier, RANKS - 1 + len(ring))

    def near(a, f, k):
        source, target, base = arrays[a]
        return pltpu.make_async_remote_copy(
            src_ref=source.at[lax.rem(rank + k, RANKS), f],
            dst_ref=target.at[f, pl.ds(base + at, rows)],
            send_sem=sends.at[a, f, k - 1],
            recv_sem=recvs.at[a, f, k - 1],
            device_id=near_id(k),
            device_id_type=MESH,
        )

    def local(a, f):
        source, target, base = arrays[a]
        return pltpu.make_async_copy(
            source.at[rank, f], target.at[f, pl.ds(base + at, rows)], local_sems.at[a, f]
        )

    def far(a, f, h):
        step, size = halos[h]
        target = arrays[a][1]
        if a == 0:
            start = reach - (step - 1) * own - size
            src, dst, other = pl.ds(reach + own - size, size), pl.ds(start, size), me + step * RANKS
        else:
            src, dst, other = pl.ds(0, size), pl.ds(step * own, size), me - step * RANKS
        return pltpu.make_async_remote_copy(
            src_ref=target.at[f, src],
            dst_ref=target.at[f, dst],
            send_sem=far_sends.at[a, f, h],
            recv_sem=far_recvs.at[a, f, h],
            device_id={"seq": other, "head": head},
            device_id_type=MESH,
        )

    def gives(a, h):
        step = halos[h][0]
        return team + step < teams if a == 0 else team - step >= 0

    def takes(a, h):
        step = halos[h][0]
        return team - step >= 0 if a == 0 else team + step < teams

    def back(a, f, k):
        source, target = returns[a]
        to = lax.rem(rank + k, RANKS)
        return pltpu.make_async_remote_copy(
            src_ref=source.at[f, pl.ds(pl.multiple_of(to * rows, rows), rows)],
            dst_ref=target.at[rank, f],
            send_sem=out_sends.at[a, f, k - 1],
            recv_sem=out_recvs.at[a, f, k - 1],
            device_id=near_id(k),
            device_id_type=MESH,
        )

    def back_local(a, f):
        source, target = returns[a]
        return pltpu.make_async_copy(
            source.at[f, pl.ds(at, rows)], target.at[rank, f], out_local.at[a, f]
        )

    def sum_copy(i, f):
        return pltpu.make_async_remote_copy(
            src_ref=grad.at[f],
            dst_ref=slots.at[i, f],
            send_sem=g_sends.at[i, f],
            recv_sem=g_recvs.at[i, f],
            device_id=mate(*ring[i]),
            device_id_type=MESH,
        )

    def share(k):
        return pltpu.make_async_remote_copy(
            src_ref=grad_all.at[rank],
            dst_ref=grad_all.at[rank],
            send_sem=s_sends.at[k - 1],
            recv_sem=s_recvs.at[k - 1],
            device_id=near_id(k),
            device_id_type=MESH,
        )

    def set_out(f):
        for a in range(2):
            for k in range(1, RANKS):
                near(a, f, k).start()
            local(a, f).start()

    for f in range(min(2, per_rank)):
        set_out(f)
    grad[...] = jnp.zeros_like(grad)
    for f in range(per_rank):
        for a in range(2):
            local(a, f).wait()
            for k in range(1, RANKS):
                near(a, f, k).wait_recv()
            for h in range(len(halos)):
                pl.when(gives(a, h))(lambda: far(a, f, h).start())
        if f + 2 < per_rank:
            set_out(f + 2)
        for taps, strip in ((past_taps, tp), (fore_taps, tf)):
            lines_all = jnp.broadcast_to(taps[f], (BLK, span))
            turned = pltpu.roll(lines_all, 0, 1, stride=1, stride_axis=0)
            strip[f] = turned.astype(jnp.bfloat16)

    i0 = lax.broadcasted_iota(jnp.int32, (BLK, BLK), 0)
    i1 = lax.broadcasted_iota(jnp.int32, (BLK, BLK), 1)
    mirror = (i0 + i1 == BLK - 1).astype(jnp.bfloat16)

    @pl.loop(0, per_rank)
    def _(f):
        for a in range(2):
            for h in range(len(halos)):
                pl.when(takes(a, h))(lambda: far(a, f, h).wait_recv())
        g_ref[...] = jnp.zeros_like(g_ref)

        @pl.loop(0, own // (2 * BLK))
        def _(pair):
            starts = [pl.multiple_of(pair * 2 * BLK + i * BLK, BLK) for i in range(2)]
            place = lax.broadcasted_iota(jnp.int32, (used, cols), 0)
            xs, ys, ss = [], [], []
            for i in range(2):
                low = used - back_len[pair * 2 + i] * BLK
                high = fore_len[pair * 2 + i] * BLK
                x = past[f, pl.ds(starts[i], used)]
                xs.append(jnp.where(place >= low, x, jnp.zeros_like(x)))
                y = future[f, pl.ds(starts[i], used)]
                ys.append(jnp.where(place < high, y, jnp.zeros_like(y)))
                ss.append(y[:BLK])
            x2, y2, s2 = [jnp.concatenate(parts, 1) for parts in (xs, ys, ss)]
            ahead = jnp.dot(tp[f, :, :used], x2, preferred_element_type=jnp.float32)
            after = jnp.dot(tf[f, :, :used], y2, preferred_element_type=jnp.float32)
            flipped = jnp.dot(mirror, s2, preferred_element_type=jnp.float32)
            g_ref[:, :used] += lax.dot_general(
                flipped.astype(jnp.bfloat16),
                x2,
                (((1,), (1,)), ((), ())),
                preferred_element_type=jnp.float32,
            )
            for i in range(2):
                part = slice(i * cols, (i + 1) * cols)
                conv[f, pl.ds(starts[i], BLK)] = ahead[:, part].astype(jnp.bfloat16)
                adj[f, pl.ds(starts[i], BLK)] = after[:, part].astype(jnp.bfloat16)

        for a in range(2):
            for k in range(1, RANKS):
                back(a, f, k).start()
            back_local(a, f).start()
        aligned = pltpu.roll(g_ref[...], 0, 1, stride=1, stride_axis=0)
        sums = jnp.sum(aligned, 0, keepdims=True)
        for c in range(used // BLK):
            grad[f, c : c + 1] = sums[:, c * BLK : (c + 1) * BLK]
        for i in range(len(ring)):
            sum_copy(i, f).start()

    for i in range(len(ring)):
        for f in range(per_rank):
            sum_copy(i, f).wait_recv()
    total = grad[...]
    for i in range(len(ring)):
        total = total + slots[i]
    grad_all[rank] = total
    for k in range(1, RANKS):
        share(k).start()
    for f in range(per_rank):
        for a in range(2):
            for k in range(1, RANKS):
                near(a, f, k).wait_send()
            for h in range(len(halos)):
                pl.when(gives(a, h))(lambda: far(a, f, h).wait_send())
        for i in range(len(ring)):
            sum_copy(i, f).wait_send()
        for a in range(2):
            back_local(a, f).wait()
            for k in range(1, RANKS):
                back(a, f, k).wait()
    for k in range(1, RANKS):
        share(k).wait()


def mix(back_len, fore_len, past_taps, fore_taps, product, scaled, teams, heads, lines):
    _, per_rank, rows, cols = product.shape
    own = RANKS * rows
    span = past_taps.shape[2]
    reach = span - 2 * BLK
    others = teams * heads - 1
    halos = len(halo_parts(own, reach))
    vmem = pl.BlockSpec(memory_space=pltpu.VMEM)
    smem = pl.BlockSpec(memory_space=pltpu.SMEM)
    dma = pltpu.SemaphoreType.DMA
    out = jax.ShapeDtypeStruct((RANKS, per_rank, rows, cols), jnp.bfloat16)
    held = pltpu.VMEM((per_rank, own + reach, cols), jnp.bfloat16)
    strip = pltpu.VMEM((per_rank, BLK, span), jnp.bfloat16)
    result = pltpu.VMEM((per_rank, own, cols), jnp.bfloat16)
    grads = (per_rank, lines, BLK)
    return pl.pallas_call(
        functools.partial(mix_kernel, teams, heads, reach),
        in_specs=[smem, smem, vmem, vmem, ANY, ANY],
        out_specs=[ANY, ANY, vmem],
        out_shape=[out, out, jax.ShapeDtypeStruct((RANKS,) + grads, jnp.float32)],
        scratch_shapes=[
            held,
            held,
            strip,
            strip,
            pltpu.VMEM((BLK, span), jnp.float32),
            result,
            result,
            pltpu.VMEM(grads, jnp.float32),
            pltpu.VMEM((others,) + grads, jnp.float32),
            dma((2, per_rank, RANKS - 1)),
            dma((2, per_rank, RANKS - 1)),
            dma((2, per_rank, halos)),
            dma((2, per_rank, halos)),
            dma((2, per_rank, RANKS - 1)),
            dma((2, per_rank, RANKS - 1)),
            dma((others, per_rank)),
            dma((others, per_rank)),
            dma((RANKS - 1,)),
            dma((RANKS - 1,)),
            dma((2, per_rank)),
            dma((2, per_rank)),
        ],
        compiler_params=pltpu.CompilerParams(
            collective_id=0, has_side_effects=True, vmem_limit_bytes=56 << 20
        ),
    )(back_len, fore_len, past_taps, fore_taps, product, scaled)


def per_device(value_rows, key_rows, query_rows, cotangent, filter_taps, doc_blocks):
    rows, channels = value_rows.shape
    filters, taps_total = filter_taps.shape
    cols = channels // filters
    per_rank = filters // RANKS
    seq, heads = lax.axis_size("seq"), lax.axis_size("head")
    teams = seq // RANKS
    own = RANKS * rows
    own_blocks = own // BLK
    lags = min(MOST, taps_total // BLK)
    used = lags * BLK
    me = lax.axis_index("seq")
    rank, team = lax.rem(me, RANKS), lax.div(me, RANKS)

    product, scaled = prepare(value_rows, key_rows, query_rows, cotangent, filters)
    shape = (RANKS, per_rank, rows, cols)
    mine = lax.dynamic_slice_in_dim(filter_taps, rank * per_rank, per_rank, 0)[:, :used]
    mine = mine.astype(jnp.bfloat16).astype(jnp.float32)
    turned = mine[:, ::-1]
    gap = jnp.zeros((per_rank, BLK), jnp.float32)
    past_taps = jnp.concatenate([turned[:, BLK - 1 :], gap, turned[:, : BLK - 1]], 1)
    fore_taps = jnp.concatenate([mine, gap], 1)

    fill = jnp.full((lags - 1,), -1, jnp.int32)
    docs = jnp.concatenate([fill, doc_blocks, fill - 1], 0)
    window = lax.dynamic_slice_in_dim(docs, team * own_blocks, own_blocks + 2 * (lags - 1))
    here = window[lags - 1 : lags - 1 + own_blocks]
    back_len = sum(
        (window[lags - 1 - b : lags - 1 - b + own_blocks] == here).astype(jnp.int32)
        for b in range(lags)
    )
    fore_len = sum(
        (window[lags - 1 + b : lags - 1 + b + own_blocks] == here).astype(jnp.int32)
        for b in range(lags)
    )
    conv_all, adj_all, grad_all = mix(
        back_len, fore_len, past_taps[:, None], fore_taps[:, None],
        product.reshape(shape), scaled.reshape(shape), teams, heads, taps_total // BLK,
    )
    whole = (filters, rows, cols)
    outs = finish(
        conv_all.reshape(whole), adj_all.reshape(whole), value_rows, key_rows, query_rows, cotangent
    )
    taps_grad = grad_all.reshape(filters, taps_total)[:, :used][:, ::-1]
    taps_grad = jnp.pad(taps_grad, ((0, 0), (0, taps_total - used)))
    return (*outs, taps_grad * (1.0 / (rows * seq)))


def solution(mesh):
    rows = P("seq", "head")
    return jax.shard_map(
        per_device,
        mesh=mesh,
        in_specs=(rows, rows, rows, rows, P(), P()),
        out_specs=(rows, rows, rows, rows, P()),
        check_vma=False,
    )
```
